128 devices in a mesh: dp: 32 (over x, y_lo, z), tensor: 4 (over y_hi, core).
Axes of the slice: x: 4, y: 4 (y_hi: 2, y_lo: 2; y = y_hi * 2 + y_lo), z: 4, core: 2. Of those that a mesh axis runs over, the one named last changes fastest.
Arguments:
- queries: bfloat16 [768, 32, 128], P('dp'), as said below
- passages: bfloat16 [768, 128, 128], P('dp', 'tensor'), as said below
- positives: int32 [768], P('dp'), may hold values from 0 to 767
Outputs:
- query_grad: float32 [768, 32, 128], P('dp')
- passage_grad: float32 [768, 128, 128], P('dp', 'tensor')
- loss: float32 [], replicated
The draws below stay inside these ranges and needn't reach their ends.
Inputs may be any that keep to these rules, and one draw needn't show every extreme that they name: `queries`: Real-valued token vectors. `passages`: Real-valued token vectors.
All inputs are finite; a program needn't handle non-finite values.
Results may differ from the reference program's by a relative error of at most 0.0029.
Values may be sent and summed in bfloat16 or wider, within the bound.
No kernel may reach another device: no remote copies, remote signals or barrier semaphores. Data moves between devices by JAX's collectives and lax.ppermute only.
A program may use at most 192 MiB of HBM per device.

```python
import jax
import jax.numpy as jnp
from jax import lax

DIM = 128
QTOK = 32
PTOK = 128
BATCH_DEV = 24
QUERIES = 768
PASSAGES = 768
N_DP = 32


def passage_base(key):
    values = jax.random.normal(key, (PASSAGES, PTOK, DIM), jnp.float32) * 0.25
    values = jnp.clip(values, -1.5, 1.5)
    return values.at[:, 0, :].set(values[:, 0, :])


def draw_passages(key, part):
    base = passage_base(key)
    return base.astype(jnp.bfloat16)


def draw_queries(key, part):
    base = passage_base(key)
    key = jax.random.fold_in(key, 7)
    values = jnp.clip(jax.random.normal(key, (QUERIES, QTOK, DIM), jnp.float32) * 0.25, -1.5, 1.5)
    rows = jnp.arange(QUERIES, dtype=jnp.int32)
    strength = 2.0 + 6.0 * rows.astype(jnp.float32) / QUERIES
    aligned = rows % 8 == 0
    first = jnp.where(aligned[:, None], strength[:, None] * base[:, 0, :], values[:, 0, :])
    values = values.at[:, 0, :].set(first)
    return values.astype(jnp.bfloat16)


def with_ends(result, rng, smallest, high):
    extent = result.shape
    place = [jax.random.randint(jax.random.fold_in(rng, axis), (), 0, extent[axis]) for axis in range(len(extent))]
    result = result.at[tuple(place)].set(smallest)
    longest = extent.index(max(extent))
    place[longest] = (place[longest] + 1) % extent[longest]
    return result.at[tuple(place)].set(high)


def setup_inputs(seed: int = 0) -> dict:
    key_list = jax.random.split(jax.random.key(seed), 4)
    return {
        "queries": draw_queries(jax.random.fold_in(key_list[3], 71), 0),
        "passages": draw_passages(jax.random.fold_in(key_list[3], 71), 0),
        "positives": with_ends(jax.random.randint(key_list[2], (QUERIES,), 0, PASSAGES), jax.random.fold_in(key_list[2], 1), 0, PASSAGES - 1).astype(jnp.int32),
    }


sharpness = 4.0
softness = 0.25


def token_logsumexp(block, passage_vectors):
    sims = jnp.einsum('qid,pjd->qipj', block, passage_vectors) * sharpness
    top = jnp.max(sims, axis=3, keepdims=True)
    return top[..., 0] + jnp.log(jnp.sum(jnp.exp(sims - top), axis=3))


def reference(queries, passages, positives):
    query_vectors = queries.astype(jnp.float32)
    passage_vectors = passages.astype(jnp.float32)
    query_blocks = query_vectors.reshape(N_DP, BATCH_DEV, QTOK, DIM)
    token_lse = lax.map(lambda block: token_logsumexp(block, passage_vectors), query_blocks)
    scores = (softness * jnp.sum(token_lse, axis=2)).reshape(QUERIES, PASSAGES)
    top = jnp.max(scores, axis=1, keepdims=True)
    row_lse = top[:, 0] + jnp.log(jnp.sum(jnp.exp(scores - top), axis=1))
    column_ids = jnp.arange(PASSAGES, dtype=jnp.int32)
    hit = column_ids[None, :] == positives[:, None]
    positive_score = jnp.sum(jnp.where(hit, scores, 0.0), axis=1)
    loss = jnp.mean(row_lse - positive_score)
    score_grad = jnp.exp(scores - row_lse[:, None]) - hit.astype(jnp.float32)
    grad_blocks = score_grad.reshape(N_DP, BATCH_DEV, PASSAGES)

    def step(carry, inputs):
        block, lse_block, grad_block = inputs
        sims = jnp.einsum('qid,pjd->qipj', block, passage_vectors) * sharpness
        weights = jnp.exp(sims - lse_block[..., None])
        mixed = (grad_block[:, None, :, None] * weights).astype(jnp.bfloat16).astype(jnp.float32)
        query_part = jnp.einsum('qipj,pjd->qid', mixed, passage_vectors)
        carry = carry + jnp.einsum('qipj,qid->pjd', mixed, block)
        return carry, query_part

    start = jnp.zeros((PASSAGES, PTOK, DIM), jnp.float32)
    passage_grad, query_parts = lax.scan(step, start, (query_blocks, token_lse, grad_blocks))
    query_grad = query_parts.reshape(QUERIES, QTOK, DIM)
    return query_grad, passage_grad, loss
```

```python
import jax
import jax.numpy as jnp
import numpy as np
from jax import lax
from jax.experimental import pallas as pl
from jax.experimental.pallas import tpu as pltpu
from jax.sharding import Mesh
from jax.sharding import PartitionSpec as P

sharpness = 4.0
to_base2 = sharpness * float(np.log2(np.e))
f32 = jnp.float32
bf16 = jnp.bfloat16

chunks = (8, 4)
peers = 8
span = 24
tokens = 32
ptok = 128
dim = 128
extra = 16
lane_tile = 256
block = 1024

nt = (((1,), (1,)), ((), ()))
params = pltpu.CompilerParams(vmem_limit_bytes=56 * 2**20)


def load_queries(qin, qs):
    rows = qin.shape[1] - extra
    for peer in range(peers):
        qs[peer * rows : (peer + 1) * rows, :] = qin[peer, :rows, :]


def load_passages(pin, ps):
    for x in range(4):
        for k in range(6):
            for part in range(4):
                row = (x * 6 + k) * ptok + part * tokens
                ps[row : row + tokens, :] = pin[x * 4 + part, k * tokens : (k + 1) * tokens, :]


def load_positives(qin, out):
    rows = qin.shape[1] - extra
    width = rows // dim
    for peer in range(peers):
        tail = qin[peer, rows : rows + extra, :].astype(f32)
        for piece in range(width):
            start = peer * rows + piece * dim
            out[0:1, start : start + dim] = (
                tail[piece : piece + 1] * 32.0 + tail[8 + piece : 9 + piece]
            )


def group_sum(values, ones):
    high = values.astype(bf16)
    rest = values - high.astype(f32)
    middle = rest.astype(bf16)
    low = (rest - middle.astype(f32)).astype(bf16)
    dot = lambda part: jnp.dot(part, ones, preferred_element_type=f32)
    return dot(high) + (dot(middle) + dot(low))


def forward_kernel(first, *refs):
    if first:
        qin, pin, ids, lse, scores, part, qs, ps, pos, ones = refs
    else:
        qin, pin, ids, before, lse, scores, part, qs, ps, pos, ones = refs
    load_queries(qin, qs)
    load_passages(pin, ps)
    load_positives(qin, pos)
    groups = [
        lax.shift_right_logical(lax.broadcasted_iota(jnp.int32, ones.shape, axis), 5)
        for axis in (0, 1)
    ]
    ones[...] = (groups[0] == groups[1]).astype(f32).astype(bf16)

    @pl.loop(0, qs.shape[0] // lane_tile)
    def _(number):
        here = pl.ds(pl.multiple_of(number * lane_tile, lane_tile), lane_tile)
        tile = qs[here, :]
        for i in range(span):
            sims = lax.dot_general(
                ps[i * ptok : (i + 1) * ptok, :], tile, nt, preferred_element_type=f32
            )
            top = jnp.max(sims, axis=0, keepdims=True)
            total = jnp.sum(jnp.exp2((sims - top) * to_base2), axis=0, keepdims=True)
            lse[i : i + 1, here] = top + jnp.log(total) * (1.0 / sharpness)
        summed = group_sum(lse[:, here], ones[...])
        scores[:, here] = summed
        hit = pos[0:1, here] == ids[...]
        positive = jnp.sum(jnp.where(hit, summed, 0.0), axis=0, keepdims=True)
        top = jnp.max(summed, axis=0, keepdims=True)
        if not first:
            top = jnp.maximum(top, before[0, 0:1, here])
            positive = positive + before[0, 1:2, here]
        total = jnp.sum(jnp.exp(summed - top), axis=0, keepdims=True)
        if not first:
            total = total + jnp.exp(before[0, 0:1, here] - top)
        row = top + jnp.log(total)
        for peer in range(part.shape[0]):
            part[peer, 0:1, here] = row
            part[peer, 1:2, here] = positive


def forward(qin, pin, ids, before):
    lanes = peers * (qin.shape[1] - extra)
    first = before is None
    copies = 1 if first else 16
    shapes = [(span, lanes), (span, lanes), (copies, 2, lanes)]
    ops = (qin, pin, ids) if first else (qin, pin, ids, before)
    return pl.pallas_call(
        lambda *refs: forward_kernel(first, *refs),
        out_shape=[jax.ShapeDtypeStruct(s, f32) for s in shapes],
        scratch_shapes=[
            pltpu.VMEM((lanes, dim), bf16),
            pltpu.VMEM((span * ptok, dim), bf16),
            pltpu.VMEM((1, lanes), f32),
            pltpu.VMEM((lane_tile, lane_tile), bf16),
        ],
        compiler_params=params,
        cost_estimate=pl.CostEstimate(
            flops=lanes * span * ptok * dim * 2,
            bytes_accessed=4 * 2**20,
            transcendentals=lanes * span * ptok,
        ),
    )(*ops)


def backward_kernel(has_pg, has_qg, *refs):
    refs = list(refs)
    qin, pin, ids, lse, scores, gathered = refs[:6]
    del refs[:6]
    pg_in = refs.pop(0) if has_pg else None
    qg_in = refs.pop(0) if has_qg else None
    pg, qg, loss, qs, ps, pt, pos, grad, mixed = refs
    load_queries(qin, qs)
    load_passages(pin, ps)
    load_positives(qin, pos)
    pt[...] = ps[...].T
    rows = gathered[:, 0, :]
    top = jnp.max(rows, axis=0, keepdims=True)
    row_lse = top + jnp.log(jnp.sum(jnp.exp(rows - top), axis=0, keepdims=True))
    positive = jnp.sum(gathered[:, 1, :], axis=0, keepdims=True)
    loss[...] = jnp.broadcast_to(jnp.sum(row_lse - positive, axis=1, keepdims=True), loss.shape)
    hit = (pos[...] == ids[...]).astype(f32)
    grad[...] = jnp.exp(scores[...] - row_lse) - hit
    if has_pg:
        pg[...] = pg_in[...]
    else:
        pg[...] = jnp.zeros_like(pg)

    @pl.loop(0, qs.shape[0] // block)
    def _(number):
        for part in range(block // lane_tile):
            here = pl.ds(
                pl.multiple_of(number * block + part * lane_tile, lane_tile), lane_tile
            )
            tile = qs[here, :]
            for i in range(span):
                sims = lax.dot_general(
                    ps[i * ptok : (i + 1) * ptok, :], tile, nt, preferred_element_type=f32
                )
                weights = jnp.exp2((sims - lse[i : i + 1, here]) * to_base2)
                mixed[i * ptok : (i + 1) * ptok, part * lane_tile : (part + 1) * lane_tile] = (
                    weights * grad[i : i + 1, here]
                ).astype(bf16)
        whole = pl.ds(pl.multiple_of(number * block, block), block)
        pg[...] += jnp.dot(mixed[...], qs[whole, :], preferred_element_type=f32)
        terms = jnp.dot(pt[...], mixed[...], preferred_element_type=f32).T
        if has_qg:
            terms = terms + qg_in[whole, :]
        qg[whole, :] = terms.astype(qg.dtype)


def backward(qin, pin, ids, lse, scores, gathered, pg_in, qg_in):
    lanes = peers * (qin.shape[1] - extra)
    ops = [qin, pin, ids, lse, scores, gathered]
    ops += [v for v in (pg_in, qg_in) if v is not None]
    return pl.pallas_call(
        lambda *refs: backward_kernel(pg_in is not None, qg_in is not None, *refs),
        out_shape=[
            jax.ShapeDtypeStruct((span * ptok, dim), f32),
            jax.ShapeDtypeStruct((lanes, dim), f32 if qg_in is None else bf16),
            jax.ShapeDtypeStruct((8, dim), f32),
        ],
        scratch_shapes=[
            pltpu.VMEM((lanes, dim), bf16),
            pltpu.VMEM((span * ptok, dim), bf16),
            pltpu.VMEM((dim, span * ptok), bf16),
            pltpu.VMEM((1, lanes), f32),
            pltpu.VMEM((span, lanes), f32),
            pltpu.VMEM((span * ptok, block), bf16),
        ],
        compiler_params=params,
        cost_estimate=pl.CostEstimate(
            flops=lanes * span * ptok * dim * 6,
            bytes_accessed=4 * 2**20,
            transcendentals=lanes * span * ptok,
        ),
    )(*ops)


def combine_kernel(own, other, loss, out):
    for x in range(4):
        for k in range(6):
            for part in range(4):
                row = (x * 6 + k) * ptok + part * tokens
                out[x * 4 + part, k * tokens : (k + 1) * tokens, :] = (
                    own[row : row + tokens, :] + other[row : row + tokens, :]
                ).astype(bf16)
    value = loss[...]
    high = value.astype(bf16).astype(f32)
    middle = (value - high).astype(bf16).astype(f32)
    low = value - high - middle
    which = lax.broadcasted_iota(jnp.int32, (extra, dim), 0)
    rows = jnp.where(which == 0, high[0:1], jnp.where(which == 1, middle[0:1], low[0:1]))
    for dest in range(16):
        out[dest, 6 * tokens :, :] = rows.astype(bf16)


def combine(own, other, loss):
    return pl.pallas_call(
        combine_kernel,
        out_shape=jax.ShapeDtypeStruct((16, 6 * tokens + extra, dim), bf16),
        compiler_params=params,
    )(own, other, loss)


def body(queries, passages, positives):
    core = lax.axis_index("c")
    half = lax.dynamic_slice_in_dim(queries, core * 12, 12, 0)
    half_positives = lax.dynamic_slice_in_dim(positives, core * 12, 12, 0)
    pieces = []
    start = 0
    for count in chunks:
        rows = half[start : start + count].reshape(count * tokens, dim)
        spread = jnp.repeat(half_positives[start : start + count], tokens).reshape(-1, dim)
        pad = ((0, 8 - spread.shape[0]), (0, 0))
        tail = jnp.concatenate([jnp.pad(spread // 32, pad), jnp.pad(spread % 32, pad)])
        pieces.append(jnp.concatenate([rows, tail.astype(bf16)]))
        start += count

    def spread_to(piece, count, axes):
        return lax.all_to_all(
            jnp.broadcast_to(piece[None], (count,) + piece.shape), axes, 0, 0, tiled=True
        )

    own = passages.reshape(1, 4, 6 * tokens, dim)
    own = jnp.broadcast_to(own, (4, 4, 6 * tokens, dim)).reshape(16, 6 * tokens, dim)
    own = lax.all_to_all(own, ("x", "yh", "c"), 0, 0, tiled=True)
    qins = [spread_to(piece, peers, ("yl", "z")) for piece in pieces]
    swap = ((0, 1), (1, 0))
    pins = [own, lax.ppermute(own, "c", swap)]

    place = lax.axis_index(("yl", "z")) * 24
    numbers = jnp.arange(span, dtype=jnp.int32)
    local = (numbers // 6) * 192 + numbers % 6
    ids = [
        (local + place + (lax.axis_index("yh") * 2 + side) * 6).astype(f32)[:, None]
        for side in (core, 1 - core)
    ]

    saved = []
    gathered = []
    for qin in qins:
        part = None
        tables = []
        for pin, numbers in zip(pins, ids):
            lse, scores, part = forward(qin, pin, numbers, part)
            tables.append((lse, scores))
        saved.append(tables)
        gathered.append(lax.all_to_all(part, ("yl", "z", "yh"), 0, 0, tiled=True))

    pgs = [None, None]
    losses = []
    arrived = []
    other = None
    for number, qin in enumerate(qins):
        qg = None
        for slot in (1, 0):
            lse, scores = saved[number][slot]
            pgs[slot], qg, loss = backward(
                qin, pins[slot], ids[slot], lse, scores, gathered[number], pgs[slot], qg
            )
            if slot == 1 and number == len(qins) - 1:
                other = lax.ppermute(pgs[1], "c", swap)
        losses.append(loss)
        arrived.append(
            lax.all_to_all(qg.reshape(16, -1, dim), ("yl", "z", "yh"), 0, 0, tiled=True)
        )

    payload = combine(pgs[0], other, sum(losses))
    landed = lax.all_to_all(payload, ("x", "yh", "c"), 0, 0, tiled=True)
    landed = landed.reshape(4, 4, 6 * tokens + extra, dim).astype(f32)
    passage_grad = jnp.sum(landed[:, :, : 6 * tokens], axis=0).reshape(24, tokens, dim)
    total = jnp.sum(landed[:, :2, 6 * tokens : 6 * tokens + 3, 0])
    loss = total / (768 * tokens)

    mine = jnp.concatenate([jnp.sum(a.astype(f32), axis=0) for a in arrived], axis=0)
    full = lax.all_gather(mine, ("yh", "c"), axis=0, tiled=False)
    full = full.reshape(2, 2, 6 * tokens, dim)
    parts = []
    for side in range(2):
        start = 0
        for count in chunks:
            rows = count // 2 * tokens
            parts += [full[yh, side, start : start + rows] for yh in range(2)]
            start += rows
    query_grad = jnp.concatenate(parts, axis=0).reshape(24, tokens, dim)
    return query_grad, passage_grad, loss


def solution(mesh):
    fine = Mesh(mesh.devices.reshape(4, 2, 4, 2, 2), ("x", "yl", "z", "yh", "c"))
    dp = ("x", "yl", "z")
    tensor = ("yh", "c")
    return jax.shard_map(
        body,
        mesh=fine,
        in_specs=(P(dp, None, None), P(dp, tensor, None), P(dp)),
        out_specs=(P(dp, None, None), P(dp, tensor, None), P()),
        check_vma=False,
    )
```

```python
import jax
import jax.numpy as jnp
import numpy as np
from jax import lax
from jax.experimental import pallas as pl
from jax.experimental.pallas import tpu as pltpu
from jax.sharding import Mesh
from jax.sharding import PartitionSpec as P

sharpness = 4.0
to_base2 = sharpness * float(np.log2(np.e))
f32 = jnp.float32
bf16 = jnp.bfloat16

chunks = (8, 4)
peers = 8
span = 24
tokens = 32
ptok = 128
dim = 128
extra = 16
lane_tile = 256
block = 1024

nt = (((1,), (1,)), ((), ()))
params = pltpu.CompilerParams(vmem_limit_bytes=56 * 2**20)
cost = pl.CostEstimate(flops=3 * 10**10, bytes_accessed=8 * 10**6, transcendentals=10**7)
smem = pl.BlockSpec(memory_space=pltpu.SMEM)
vmem = pl.BlockSpec(memory_space=pltpu.VMEM)


def absolute(place, peer):
    back, side = peer // 2, peer % 2
    return lax.rem(place[0] + side, 2) * 4 + lax.rem(place[1] + 4 - back, 4)


def chunk_rows(number):
    start = sum(c * tokens + extra for c in chunks[:number])
    lane = sum(c * tokens * peers for c in chunks[:number])
    return start, chunks[number] * tokens, lane


def load_queries(numbers, qins, qs, pos):
    first = chunk_rows(numbers[0])[2]
    for number in numbers:
        start, rows, lane = chunk_rows(number)
        for peer in range(peers):
            source = qins[peer % 2].at[peer // 2]
            here = lane - first + peer * rows
            qs[here : here + rows, :] = source[start : start + rows, :]
            tail = source[start + rows : start + rows + extra, :].astype(f32)
            for piece in range(rows // dim):
                pos[0:1, here + piece * dim : here + (piece + 1) * dim] = (
                    tail[piece : piece + 1] * 32.0 + tail[8 + piece : 9 + piece]
                )


def load_passages(pins, ps):
    for slot, pin in enumerate(pins):
        for x in range(4):
            for k in range(6):
                for part in range(4):
                    row = (slot * span + x * 6 + k) * ptok + part * tokens
                    ps[row : row + tokens, :] = pin[x * 4 + part, k * tokens : (k + 1) * tokens, :]


def group_sum(values, ones):
    high = values.astype(bf16)
    rest = values - high.astype(f32)
    middle = rest.astype(bf16)
    low = (rest - middle.astype(f32)).astype(bf16)
    dot = lambda part: jnp.dot(part, ones, preferred_element_type=f32)
    return dot(high) + (dot(middle) + dot(low))


def forward_kernel(slots, first, copies, *refs):
    refs = list(refs)
    place = refs.pop(0)
    qins = [refs.pop(0) for _ in range(2)]
    pins = [refs.pop(0) for _ in range(slots)]
    ids = [refs.pop(0) for _ in range(slots)]
    before = None if first else refs.pop(0)
    lses = [refs.pop(0) for _ in range(slots)]
    tables = [refs.pop(0) for _ in range(slots)]
    part, qs, ps, pos, ones, local = refs
    load_queries((0, 1), qins, qs, pos)
    load_passages(pins, ps)
    groups = [
        lax.shift_right_logical(lax.broadcasted_iota(jnp.int32, ones.shape, axis), 5)
        for axis in (0, 1)
    ]
    ones[...] = (groups[0] == groups[1]).astype(f32).astype(bf16)

    @pl.loop(0, qs.shape[0] // (2 * lane_tile))
    def _(step):
        for side in range(2):
            start = pl.multiple_of(step * (2 * lane_tile) + side * lane_tile, lane_tile)
            here = pl.ds(start, lane_tile)
            tile = qs[here, :]
            for i in range(slots * span):
                sims = lax.dot_general(
                    ps[i * ptok : (i + 1) * ptok, :], tile, nt, preferred_element_type=f32
                )
                top = jnp.max(sims, axis=0, keepdims=True)
                total = jnp.sum(jnp.exp2((sims - top) * to_base2), axis=0, keepdims=True)
                lses[i // span][i % span : i % span + 1, here] = top + jnp.log(total) * (
                    1.0 / sharpness
                )

    for tile in range(qs.shape[0] // lane_tile):
        here = slice(tile * lane_tile, (tile + 1) * lane_tile)
        positive = top = None
        for slot in range(slots):
            summed = group_sum(lses[slot][:, here], ones[...])
            tables[slot][:, here] = summed
            hit = pos[0:1, here] == ids[slot][...]
            found = jnp.sum(jnp.where(hit, summed, 0.0), axis=0, keepdims=True)
            most = jnp.max(summed, axis=0, keepdims=True)
            positive = found if slot == 0 else positive + found
            top = most if slot == 0 else jnp.maximum(top, most)
        if not first:
            top = jnp.maximum(top, before[0:1, here])
            positive = positive + before[1:2, here]
        total = jnp.exp(before[0:1, here] - top) if not first else 0.0
        for slot in range(slots):
            total = total + jnp.sum(jnp.exp(tables[slot][:, here] - top), axis=0, keepdims=True)
        local[0:1, here] = top + jnp.log(total)
        local[1:2, here] = positive

    if copies == 1:
        part[...] = local[...]
    else:
        for number in range(len(chunks)):
            _, rows, lane = chunk_rows(number)
            for peer in range(peers):
                start = lane + absolute(place, peer) * rows
                there = pl.ds(pl.multiple_of(start, rows), rows)
                for copy in range(copies):
                    part[copy, :, there] = local[:, lane + peer * rows : lane + (peer + 1) * rows]


def forward(place, qins, pins, ids, before, copies):
    lanes = peers * sum(chunks) * tokens
    slots = len(pins)
    first = before is None
    shapes = [(span, lanes)] * (2 * slots)
    shapes.append((2, lanes) if copies == 1 else (copies, 2, lanes))
    ops = [place, *qins, *pins, *ids] + ([] if first else [before])
    outs = pl.pallas_call(
        lambda *refs: forward_kernel(slots, first, copies, *refs),
        out_shape=[jax.ShapeDtypeStruct(s, f32) for s in shapes],
        in_specs=[smem] + [vmem] * (len(ops) - 1),
        scratch_shapes=[
            pltpu.VMEM((lanes, dim), bf16),
            pltpu.VMEM((slots * span * ptok, dim), bf16),
            pltpu.VMEM((1, lanes), f32),
            pltpu.VMEM((lane_tile, lane_tile), bf16),
            pltpu.VMEM((2, lanes), f32),
        ],
        compiler_params=params,
        cost_estimate=cost,
    )(*ops)
    return outs[:slots], outs[slots : 2 * slots], outs[-1]


def backward_kernel(number, slots, has_pg, has_qg, has_loss, doubled, *refs):
    refs = list(refs)
    place = refs.pop(0)
    qins = [refs.pop(0) for _ in range(2)]
    pins = [refs.pop(0) for _ in range(slots)]
    ids = [refs.pop(0) for _ in range(slots)]
    lses = [refs.pop(0) for _ in range(slots)]
    tables = [refs.pop(0) for _ in range(slots)]
    gathered = refs.pop(0)
    pg_in = refs.pop(0) if has_pg else None
    qg_in = refs.pop(0) if has_qg else None
    loss_in = refs.pop(0) if has_loss else None
    pgs = [refs.pop(0) for _ in range(slots)]
    qg, loss, qs, ps, pt, pos, grad, mixed, gap = refs
    load_queries((number,), qins, qs, pos)
    load_passages(pins, ps)
    pt[...] = ps[...].T
    rows = chunk_rows(number)[1]
    _, rows, lane = chunk_rows(number)
    for peer in range(peers):
        there = pl.ds(pl.multiple_of(lane + absolute(place, peer) * rows, rows), rows)
        here = slice(peer * rows, (peer + 1) * rows)
        parts = gathered[:, 0, there]
        top = jnp.max(parts, axis=0, keepdims=True)
        row_lse = top + jnp.log(jnp.sum(jnp.exp(parts - top), axis=0, keepdims=True))
        positive = jnp.sum(gathered[:, 1, there], axis=0, keepdims=True)
        ordered = pl.ds(pl.multiple_of(absolute(place, peer) * rows, rows), rows)
        gap[0:1, ordered] = row_lse - positive
        for slot in range(slots):
            hit = (pos[0:1, here] == ids[slot][...]).astype(f32)
            lines = slice(slot * span, (slot + 1) * span)
            score = tables[slot][:, lane + peer * rows : lane + (peer + 1) * rows]
            grad[lines, here] = jnp.exp(score - row_lse) - hit
    value = jnp.sum(gap[...], axis=1, keepdims=True)
    loss[...] = jnp.broadcast_to(value, loss.shape)
    if has_loss:
        loss[...] += loss_in[...]
    for pg in pgs:
        pg[...] = pg_in[...] if has_pg else jnp.zeros_like(pg)

    @pl.loop(0, qs.shape[0] // block)
    def _(step):
        for piece in range(block // lane_tile):
            here = pl.ds(pl.multiple_of(step * block + piece * lane_tile, lane_tile), lane_tile)
            there = pl.ds(
                pl.multiple_of(lane + step * block + piece * lane_tile, lane_tile), lane_tile
            )
            tile = qs[here, :]
            for i in range(slots * span):
                sims = lax.dot_general(
                    ps[i * ptok : (i + 1) * ptok, :], tile, nt, preferred_element_type=f32
                )
                row = lses[i // span][i % span : i % span + 1, there]
                weights = jnp.exp2((sims - row) * to_base2)
                mixed[i * ptok : (i + 1) * ptok, piece * lane_tile : (piece + 1) * lane_tile] = (
                    weights * grad[i : i + 1, here]
                ).astype(bf16)
        whole = pl.ds(pl.multiple_of(step * block, block), block)
        for slot, pg in enumerate(pgs):
            lines = slice(slot * span * ptok, (slot + 1) * span * ptok)
            pg[...] += jnp.dot(mixed[lines, :], qs[whole, :], preferred_element_type=f32)
        terms = jnp.dot(pt[...], mixed[...], preferred_element_type=f32).T
        if has_qg:
            terms = terms + qg_in[whole, :]
        if doubled:
            for part in range(block // rows):
                start = absolute(place, step * (block // rows) + part) * (2 * rows)
                piece = terms[part * rows : (part + 1) * rows].astype(qg.dtype)
                for copy in range(2):
                    qg[pl.ds(pl.multiple_of(start + copy * rows, rows), rows), :] = piece
        else:
            qg[whole, :] = terms.astype(qg.dtype)


def backward(number, place, qins, pins, ids, lses, tables, gathered, before, doubled, kind):
    lanes = peers * chunk_rows(number)[1]
    slots = len(pins)
    ops = [place, *qins, *pins, *ids, *lses, *tables, gathered] + [v for v in before if v is not None]
    flags = [v is not None for v in before] + [doubled]
    outs = pl.pallas_call(
        lambda *refs: backward_kernel(number, slots, *flags, *refs),
        out_shape=[jax.ShapeDtypeStruct((span * ptok, dim), f32)] * slots
        + [
            jax.ShapeDtypeStruct((2 * lanes if doubled else lanes, dim), kind),
            jax.ShapeDtypeStruct((8, dim), f32),
        ],
        in_specs=[smem] + [vmem] * (len(ops) - 1),
        scratch_shapes=[
            pltpu.VMEM((lanes, dim), bf16),
            pltpu.VMEM((slots * span * ptok, dim), bf16),
            pltpu.VMEM((dim, slots * span * ptok), bf16),
            pltpu.VMEM((1, lanes), f32),
            pltpu.VMEM((slots * span, lanes), f32),
            pltpu.VMEM((slots * span * ptok, block), bf16),
            pltpu.VMEM((1, lanes), f32),
        ],
        compiler_params=params,
        cost_estimate=cost,
    )(*ops)
    return outs[:slots], outs[slots], outs[slots + 1]


def combine_kernel(own, other, loss_own, loss_other, *outs):
    for x in range(4):
        out = outs[x]
        for k in range(6):
            for part in range(4):
                row = (x * 6 + k) * ptok + part * tokens
                there = part * 6 * tokens + k * tokens
                out[there : there + tokens, :] = (
                    own[row : row + tokens, :] + other[row : row + tokens, :]
                ).astype(out.dtype)
    value = loss_own[...] + loss_other[...]
    high = value.astype(bf16).astype(f32)
    middle = (value - high).astype(bf16).astype(f32)
    low = value - high - middle
    which = lax.broadcasted_iota(jnp.int32, (extra, dim), 0)
    rows = jnp.where(which == 0, high[0:1], jnp.where(which == 1, middle[0:1], low[0:1]))
    for out in outs:
        out[4 * 6 * tokens :, :] = rows.astype(out.dtype)


def combine(own, other, loss_own, loss_other):
    rows = 4 * 6 * tokens + extra
    return pl.pallas_call(
        combine_kernel,
        out_shape=[jax.ShapeDtypeStruct((rows, dim), f32 if x == 0 else bf16) for x in range(4)],
        in_specs=[vmem] * 4,
        compiler_params=params,
        cost_estimate=cost,
    )(own, other, loss_own, loss_other)


def exchange(value, axes, step):
    size = 4 if isinstance(axes, tuple) else 2
    return lax.ppermute(value, axes, [(i, i ^ step) for i in range(size)])


def rotate(value, step):
    return lax.ppermute(value, "x", [(i, (i + step) % 4) for i in range(4)])


def by_tensor(blocks, yh, core):
    a, b, c, d = blocks
    a, b = jnp.where(core == 0, a, b), jnp.where(core == 0, b, a)
    c, d = jnp.where(core == 0, c, d), jnp.where(core == 0, d, c)
    low = [jnp.where(yh == 0, u, v) for u, v in ((a, c), (b, d), (c, a), (d, b))]
    return jnp.concatenate(low)


def body(queries, passages, positives):
    core, yh, yl, z, x = (lax.axis_index(a) for a in ("c", "yh", "yl", "z", "x"))
    spot = yh * 2 + core
    both = ("yh", "c")
    group = ("yl", "z", "yh")

    half = lax.dynamic_slice_in_dim(queries, core * 12, 12, 0)
    half_positives = lax.dynamic_slice_in_dim(positives, core * 12, 12, 0)
    pieces = []
    start = 0
    for count in chunks:
        rows = half[start : start + count].reshape(count * tokens, dim)
        spread = jnp.repeat(half_positives[start : start + count], tokens).reshape(-1, dim)
        pad = ((0, 8 - spread.shape[0]), (0, 0))
        tail = jnp.concatenate([jnp.pad(spread // 32, pad), jnp.pad(spread % 32, pad)])
        pieces += [rows, tail.astype(bf16)]
        start += count
    piece = jnp.concatenate(pieces)
    blocks = passages.reshape(4, 6 * tokens, dim)
    part_of = lambda s: lax.dynamic_slice_in_dim(blocks, spot ^ s, 1, 0)
    quarters = [part_of(0)] + [exchange(part_of(s), both, s) for s in (1, 2, 3)]
    around = [piece] + [
        lax.ppermute(piece, "z", [(i, (i + s) % 4) for i in range(4)]) for s in (1, 2, 3)
    ]
    quarters, around = lax.optimization_barrier((quarters, around))
    quarters = jnp.concatenate(quarters)
    around = jnp.stack(around)
    own = [quarters] + [rotate(quarters, s) for s in (1, 2, 3)]
    qins = [around, exchange(around, "yl", 1)]
    own, qins = lax.optimization_barrier((own, qins))
    own = jnp.concatenate(own)
    pins = [own, exchange(own, "c", 1)]
    place = jnp.stack([yl, z]).astype(jnp.int32)

    numbers = jnp.arange(span, dtype=jnp.int32)
    local = ((x + 4 - numbers // 6) % 4) * 192 + numbers % 6 + (yl * 4 + z) * 24
    ids = [(local + (spot ^ side) * 6).astype(f32)[:, None] for side in (0, 1)]

    lse0, table0, part = forward(place, qins, pins[:1], ids[:1], None, 1)
    lse1, table1, part = forward(place, qins, pins[1:], ids[1:], part, 16)
    gathered = lax.all_to_all(part, group, 0, 0, tiled=True)

    pgs, qg, loss = backward(
        0, place, qins, pins, ids, lse0 + lse1, table0 + table1, gathered, (None,) * 3, False, bf16
    )
    qg = qg.reshape(4, 2, -1, dim)
    terms = [qg[0]] + [
        lax.ppermute(qg[s], "z", [(i, (i + 4 - s) % 4) for i in range(4)]) for s in (1, 2, 3)
    ]
    terms = [t.astype(f32) for t in terms]
    early = (terms[0] + terms[1]) + (terms[2] + terms[3])
    early = early[0] + exchange(early[1], "yl", 1)
    early = early + exchange(early, "yh", 1)

    (pg1,), qg, loss = backward(
        1, place, qins, pins[1:], ids[1:], lse1, table1, gathered, (pgs[1], None, loss), False, f32
    )
    other = exchange(pg1, "c", 1)
    loss_other = exchange(loss, "c", 1)
    (pg0,), qg, _ = backward(
        1, place, qins, pins[:1], ids[:1], lse0, table0, gathered, (pgs[0], qg, None), True, bf16
    )

    sent = combine(pg0, other, loss, loss_other)
    qg, sent = lax.optimization_barrier((qg, sent))
    arrived = lax.all_to_all(qg.reshape(16, -1, dim), group, 0, 0, tiled=True)
    landed = [sent[0]] + [rotate(sent[s], 4 - s).astype(f32) for s in (1, 2, 3)]
    summed = (landed[0] + landed[2]) + (landed[1] + landed[3])
    arrived, summed = lax.optimization_barrier((arrived, summed))
    values = [jnp.sum(part[4 * 6 * tokens : 4 * 6 * tokens + 3, 0]) for part in landed]
    loss = ((values[0] + values[2]) + (values[1] + values[3])) / (768 * tokens)

    rows = 6 * tokens
    done = jnp.concatenate([early, jnp.sum(arrived.astype(f32), axis=0)])
    sibling = exchange(done, "c", 1)
    query_grad = jnp.concatenate(
        [jnp.where(core == 0, done, sibling), jnp.where(core == 0, sibling, done)]
    ).reshape(24, tokens, dim)

    homes = [summed[:rows]] + [
        exchange(summed[s * rows : (s + 1) * rows], both, s) for s in (1, 2, 3)
    ]
    passage_grad = by_tensor(homes, yh, core).reshape(24, tokens, dim)
    return query_grad, passage_grad, loss


def solution(mesh):
    fine = Mesh(mesh.devices.reshape(4, 2, 4, 2, 2), ("x", "yl", "z", "yh", "c"))
    dp = ("x", "yl", "z")
    tensor = ("yh", "c")
    return jax.shard_map(
        body,
        mesh=fine,
        in_specs=(P(dp, None, None), P(dp, tensor, None), P(dp)),
        out_specs=(P(dp, None, None), P(dp, tensor, None), P()),
        check_vma=False,
    )
```

```python
import jax
import jax.numpy as jnp
import numpy as np
from jax import lax
from jax.experimental import pallas as pl
from jax.experimental.pallas import tpu as pltpu
from jax.sharding import Mesh
from jax.sharding import PartitionSpec as P

sharpness = 4.0
to_base2 = sharpness * float(np.log2(np.e))
f32 = jnp.float32
bf16 = jnp.bfloat16

chunks = (8, 4)
peers = 8
span = 24
tokens = 32
ptok = 128
dim = 128
extra = 16
lane_tile = 256
block = 1024

nt = (((1,), (1,)), ((), ()))
params = pltpu.CompilerParams(vmem_limit_bytes=56 * 2**20)
cost = pl.CostEstimate(flops=3 * 10**10, bytes_accessed=8 * 10**6, transcendentals=10**7)
smem = pl.BlockSpec(memory_space=pltpu.SMEM)
vmem = pl.BlockSpec(memory_space=pltpu.VMEM)


def absolute(place, peer):
    back, side = peer // 2, peer % 2
    return lax.rem(place[0] + side, 2) * 4 + lax.rem(place[1] + 4 - back, 4)


def chunk_rows(number):
    start = sum(c * tokens + extra for c in chunks[:number])
    lane = sum(c * tokens * peers for c in chunks[:number])
    return start, chunks[number] * tokens, lane


def load_queries(numbers, qins, qs, pos):
    first = chunk_rows(numbers[0])[2]
    for number in numbers:
        start, rows, lane = chunk_rows(number)
        for peer in range(peers):
            source = qins[peer % 2].at[peer // 2]
            here = lane - first + peer * rows
            qs[here : here + rows, :] = source[start : start + rows, :]
            tail = source[start + rows : start + rows + extra, :].astype(f32)
            for piece in range(rows // dim):
                pos[0:1, here + piece * dim : here + (piece + 1) * dim] = (
                    tail[piece : piece + 1] * 32.0 + tail[8 + piece : 9 + piece]
                )


def load_passages(pins, ps):
    for slot, pin in enumerate(pins):
        for x in range(4):
            for k in range(6):
                for part in range(4):
                    row = (slot * span + x * 6 + k) * ptok + part * tokens
                    ps[row : row + tokens, :] = pin[x * 4 + part, k * tokens : (k + 1) * tokens, :]


def group_sum(values, ones):
    high = values.astype(bf16)
    rest = values - high.astype(f32)
    middle = rest.astype(bf16)
    low = (rest - middle.astype(f32)).astype(bf16)
    dot = lambda part: jnp.dot(part, ones, preferred_element_type=f32)
    return dot(high) + (dot(middle) + dot(low))


def forward_kernel(slots, first, copies, *refs):
    refs = list(refs)
    place = refs.pop(0)
    qins = [refs.pop(0) for _ in range(2)]
    pins = [refs.pop(0) for _ in range(slots)]
    ids = [refs.pop(0) for _ in range(slots)]
    before = None if first else refs.pop(0)
    lses = [refs.pop(0) for _ in range(slots)]
    tables = [refs.pop(0) for _ in range(slots)]
    part, qs, ps, pos, ones, local = refs
    load_queries((0, 1), qins, qs, pos)
    load_passages(pins, ps)
    groups = [
        lax.shift_right_logical(lax.broadcasted_iota(jnp.int32, ones.shape, axis), 5)
        for axis in (0, 1)
    ]
    ones[...] = (groups[0] == groups[1]).astype(f32).astype(bf16)

    @pl.loop(0, qs.shape[0] // (2 * lane_tile))
    def _(step):
        for side in range(2):
            start = pl.multiple_of(step * (2 * lane_tile) + side * lane_tile, lane_tile)
            here = pl.ds(start, lane_tile)
            tile = qs[here, :]
            for i in range(slots * span):
                sims = lax.dot_general(
                    ps[i * ptok : (i + 1) * ptok, :], tile, nt, preferred_element_type=f32
                )
                top = jnp.max(sims, axis=0, keepdims=True)
                total = jnp.sum(jnp.exp2((sims - top) * to_base2), axis=0, keepdims=True)
                lses[i // span][i % span : i % span + 1, here] = top + jnp.log(total) * (
                    1.0 / sharpness
                )

    for tile in range(qs.shape[0] // lane_tile):
        here = slice(tile * lane_tile, (tile + 1) * lane_tile)
        positive = top = None
        for slot in range(slots):
            summed = group_sum(lses[slot][:, here], ones[...])
            tables[slot][:, here] = summed
            hit = pos[0:1, here] == ids[slot][...]
            found = jnp.sum(jnp.where(hit, summed, 0.0), axis=0, keepdims=True)
            most = jnp.max(summed, axis=0, keepdims=True)
            positive = found if slot == 0 else positive + found
            top = most if slot == 0 else jnp.maximum(top, most)
        if not first:
            top = jnp.maximum(top, before[0:1, here])
            positive = positive + before[1:2, here]
        total = jnp.exp(before[0:1, here] - top) if not first else 0.0
        for slot in range(slots):
            total = total + jnp.sum(jnp.exp(tables[slot][:, here] - top), axis=0, keepdims=True)
        local[0:1, here] = top + jnp.log(total)
        local[1:2, here] = positive

    if copies == 1:
        part[...] = local[...]
    else:
        for number in range(len(chunks)):
            _, rows, lane = chunk_rows(number)
            for peer in range(peers):
                start = lane + absolute(place, peer) * rows
                there = pl.ds(pl.multiple_of(start, rows), rows)
                for copy in range(copies):
                    part[copy, :, there] = local[:, lane + peer * rows : lane + (peer + 1) * rows]


def forward(place, qins, pins, ids, before, copies):
    lanes = peers * sum(chunks) * tokens
    slots = len(pins)
    first = before is None
    shapes = [(span, lanes)] * (2 * slots)
    shapes.append((2, lanes) if copies == 1 else (copies, 2, lanes))
    ops = [place, *qins, *pins, *ids] + ([] if first else [before])
    outs = pl.pallas_call(
        lambda *refs: forward_kernel(slots, first, copies, *refs),
        out_shape=[jax.ShapeDtypeStruct(s, f32) for s in shapes],
        in_specs=[smem] + [vmem] * (len(ops) - 1),
        scratch_shapes=[
            pltpu.VMEM((lanes, dim), bf16),
            pltpu.VMEM((slots * span * ptok, dim), bf16),
            pltpu.VMEM((1, lanes), f32),
            pltpu.VMEM((lane_tile, lane_tile), bf16),
            pltpu.VMEM((2, lanes), f32),
        ],
        compiler_params=params,
        cost_estimate=cost,
    )(*ops)
    return outs[:slots], outs[slots : 2 * slots], outs[-1]


def aligned(value, size):
    return value if isinstance(value, int) else pl.multiple_of(value, size)


def write_payload(own, other, loss_own, loss_other, outs):
    for x in range(4):
        out = outs[x]
        for k in range(6):
            for part in range(4):
                row = (x * 6 + k) * ptok + part * tokens
                there = part * 6 * tokens + k * tokens
                out[there : there + tokens, :] = (
                    own[row : row + tokens, :] + other[row : row + tokens, :]
                ).astype(out.dtype)
    value = loss_own[...] + loss_other[...]
    high = value.astype(bf16).astype(f32)
    middle = (value - high).astype(bf16).astype(f32)
    low = value - high - middle
    which = lax.broadcasted_iota(jnp.int32, (extra, dim), 0)
    rows = jnp.where(which == 0, high[0:1], jnp.where(which == 1, middle[0:1], low[0:1]))
    for out in outs:
        out[4 * 6 * tokens :, :] = rows.astype(out.dtype)


def backward_kernel(stage, numbers, *refs):
    refs = list(refs)
    place, qa, qb, pin, ids, lse, table, gathered = refs[:8]
    del refs[:8]
    qg_in = refs.pop(0) if stage > 0 else None
    if stage == 2:
        pg_in, other, loss_own, loss_other, *outs = refs[:8]
        del refs[:8]
        qg, qs, ps, pt, pos, grad, mixed, pg = refs
    elif stage == 1:
        pg, *parts_out, qs, ps, pt, pos, grad, mixed = refs
    else:
        pg, qg, loss, qs, ps, pt, pos, grad, mixed, gap = refs
    load_queries(numbers, (qa, qb), qs, pos)
    load_passages([pin], ps)
    pt[...] = ps[...].T
    first = chunk_rows(numbers[0])[2]
    for number in numbers:
        _, rows, lane = chunk_rows(number)
        for peer in range(peers):
            there = pl.ds(pl.multiple_of(lane + absolute(place, peer) * rows, rows), rows)
            here = slice(lane - first + peer * rows, lane - first + (peer + 1) * rows)
            parts = gathered[:, 0, there]
            top = jnp.max(parts, axis=0, keepdims=True)
            row_lse = top + jnp.log(jnp.sum(jnp.exp(parts - top), axis=0, keepdims=True))
            if stage == 0:
                gap[0:1, there] = row_lse - jnp.sum(gathered[:, 1, there], axis=0, keepdims=True)
            hit = (pos[0:1, here] == ids[...]).astype(f32)
            score = table[:, lane + peer * rows : lane + (peer + 1) * rows]
            grad[:, here] = jnp.exp(score - row_lse) - hit
    if stage == 0:
        value = jnp.sum(gap[...], axis=1, keepdims=True)
        loss[...] = jnp.broadcast_to(value, loss.shape)
    pg[...] = pg_in[...] if stage == 2 else jnp.zeros_like(pg)

    def work(step):
        for piece in range(block // lane_tile):
            start = aligned(step * block + piece * lane_tile, lane_tile)
            here = pl.ds(start, lane_tile)
            there = pl.ds(aligned(first + start, lane_tile), lane_tile)
            tile = qs[here, :]
            for i in range(span):
                sims = lax.dot_general(
                    ps[i * ptok : (i + 1) * ptok, :], tile, nt, preferred_element_type=f32
                )
                weights = jnp.exp2((sims - lse[i : i + 1, there]) * to_base2)
                mixed[i * ptok : (i + 1) * ptok, piece * lane_tile : (piece + 1) * lane_tile] = (
                    weights * grad[i : i + 1, here]
                ).astype(bf16)
        whole = pl.ds(aligned(step * block, block), block)
        pg[...] += jnp.dot(mixed[...], qs[whole, :], preferred_element_type=f32)
        terms = jnp.dot(pt[...], mixed[...], preferred_element_type=f32).T
        if stage > 0:
            terms = terms + qg_in[pl.ds(aligned(first + step * block, block), block), :]
        if stage == 0:
            qg[whole, :] = terms
        elif stage == 1:
            size = parts_out[0].shape[0]
            for part in range(block // size):
                parts_out[step * (block // size) + part][...] = terms[
                    part * size : (part + 1) * size
                ].astype(bf16)
        else:
            rows = chunk_rows(numbers[0])[1]
            for part in range(block // rows):
                start = absolute(place, step * (block // rows) + part) * (2 * rows)
                piece = terms[part * rows : (part + 1) * rows].astype(qg.dtype)
                for copy in range(2):
                    qg[pl.ds(pl.multiple_of(start + copy * rows, rows), rows), :] = piece

    if stage == 0:
        pl.loop(0, qs.shape[0] // block)(work)
    else:
        for step in range(qs.shape[0] // block):
            work(step)
    if stage == 2:
        write_payload(pg, other, loss_own, loss_other, outs)


def backward(stage, *ops):
    numbers = ((0, 1), (0,), (1,))[stage]
    lanes = peers * sum(chunks[n] for n in numbers) * tokens
    shape = jax.ShapeDtypeStruct
    gradient = shape((span * ptok, dim), f32)
    payload = 4 * 6 * tokens + extra
    outs = [
        [gradient, shape((lanes, dim), f32), shape((8, dim), f32)],
        [gradient] + [shape((lanes // 4, dim), bf16)] * 4,
        [shape((payload, dim), f32 if x == 0 else bf16) for x in range(4)]
        + [shape((2 * lanes, dim), bf16)],
    ][stage]
    scratch = [
        pltpu.VMEM((lanes, dim), bf16),
        pltpu.VMEM((span * ptok, dim), bf16),
        pltpu.VMEM((dim, span * ptok), bf16),
        pltpu.VMEM((1, lanes), f32),
        pltpu.VMEM((span, lanes), f32),
        pltpu.VMEM((span * ptok, block), bf16),
    ]
    if stage == 0:
        scratch.append(pltpu.VMEM((1, lanes), f32))
    if stage == 2:
        scratch.append(pltpu.VMEM((span * ptok, dim), f32))
    return pl.pallas_call(
        lambda *refs: backward_kernel(stage, numbers, *refs),
        out_shape=outs,
        in_specs=[smem] + [vmem] * (len(ops) - 1),
        scratch_shapes=scratch,
        compiler_params=params,
        cost_estimate=cost,
    )(*ops)


def exchange(value, axes, step):
    size = 4 if isinstance(axes, tuple) else 2
    return lax.ppermute(value, axes, [(i, i ^ step) for i in range(size)])


def rotate(value, step):
    return lax.ppermute(value, "x", [(i, (i + step) % 4) for i in range(4)])


def by_tensor(blocks, yh, core):
    a, b, c, d = blocks
    a, b = jnp.where(core == 0, a, b), jnp.where(core == 0, b, a)
    c, d = jnp.where(core == 0, c, d), jnp.where(core == 0, d, c)
    low = [jnp.where(yh == 0, u, v) for u, v in ((a, c), (b, d), (c, a), (d, b))]
    return jnp.concatenate(low)


def body(queries, passages, positives):
    core, yh, yl, z, x = (lax.axis_index(a) for a in ("c", "yh", "yl", "z", "x"))
    spot = yh * 2 + core
    both = ("yh", "c")
    group = ("yl", "z", "yh")

    half = lax.dynamic_slice_in_dim(queries, core * 12, 12, 0)
    half_positives = lax.dynamic_slice_in_dim(positives, core * 12, 12, 0)
    pieces = []
    start = 0
    for count in chunks:
        rows = half[start : start + count].reshape(count * tokens, dim)
        spread = jnp.repeat(half_positives[start : start + count], tokens).reshape(-1, dim)
        pad = ((0, 8 - spread.shape[0]), (0, 0))
        tail = jnp.concatenate([jnp.pad(spread // 32, pad), jnp.pad(spread % 32, pad)])
        pieces += [rows, tail.astype(bf16)]
        start += count
    piece = jnp.concatenate(pieces)
    blocks = passages.reshape(4, 6 * tokens, dim)
    part_of = lambda s: lax.dynamic_slice_in_dim(blocks, spot ^ s, 1, 0)
    quarters = [part_of(0)] + [exchange(part_of(s), both, s) for s in (1, 2, 3)]
    around = [piece] + [
        lax.ppermute(piece, "z", [(i, (i + s) % 4) for i in range(4)]) for s in (1, 2, 3)
    ]
    quarters, around = lax.optimization_barrier((quarters, around))
    quarters = jnp.concatenate(quarters)
    around = jnp.stack(around)
    own = [quarters] + [rotate(quarters, s) for s in (1, 2, 3)]
    qins = [around, exchange(around, "yl", 1)]
    own, qins = lax.optimization_barrier((own, qins))
    own = jnp.concatenate(own)
    pins = [own, exchange(own, "c", 1)]
    place = jnp.stack([yl, z]).astype(jnp.int32)

    numbers = jnp.arange(span, dtype=jnp.int32)
    local = ((x + 4 - numbers // 6) % 4) * 192 + numbers % 6 + (yl * 4 + z) * 24
    ids = [(local + (spot ^ side) * 6).astype(f32)[:, None] for side in (0, 1)]

    lse0, table0, part = forward(place, qins, pins[:1], ids[:1], None, 1)
    lse1, table1, part = forward(place, qins, pins[1:], ids[1:], part, 16)
    gathered = lax.all_to_all(part, group, 0, 0, tiled=True)

    common = (place, *qins)
    own_side = (pins[0], ids[0], *lse0, *table0, gathered)
    pg1, qg1, loss = backward(0, *common, pins[1], ids[1], *lse1, *table1, gathered)
    other = exchange(pg1, "c", 1)
    loss_other = exchange(loss, "c", 1)
    pg0, *terms = backward(1, *common, *own_side, qg1)
    terms = [terms[0]] + [
        lax.ppermute(terms[s], "z", [(i, (i + 4 - s) % 4) for i in range(4)]) for s in (1, 2, 3)
    ]
    *sent, qg = backward(2, *common, *own_side, qg1, pg0, other, loss, loss_other)

    sent, terms = lax.optimization_barrier((sent, terms))
    landed = [sent[0]] + [rotate(sent[s], 4 - s) for s in (1, 2, 3)]
    terms = [t.astype(f32).reshape(2, -1, dim) for t in terms]
    early = (terms[0] + terms[1]) + (terms[2] + terms[3])
    early = early[0] + exchange(early[1], "yl", 1)
    qg, early = lax.optimization_barrier((qg, early))
    arrived = lax.all_to_all(qg.reshape(16, -1, dim), group, 0, 0, tiled=True)
    early = early + exchange(early, "yh", 1)
    landed = [part.astype(f32) for part in landed]
    summed = (landed[0] + landed[2]) + (landed[1] + landed[3])
    loss = jnp.sum(summed[4 * 6 * tokens : 4 * 6 * tokens + 3, 0]) / (768 * tokens)

    rows = 6 * tokens
    done = jnp.concatenate([early, jnp.sum(arrived.astype(f32), axis=0)])
    sibling = exchange(done, "c", 1)
    query_grad = jnp.concatenate(
        [jnp.where(core == 0, done, sibling), jnp.where(core == 0, sibling, done)]
    ).reshape(24, tokens, dim)

    homes = [summed[:rows]] + [
        exchange(summed[s * rows : (s + 1) * rows], both, s) for s in (1, 2, 3)
    ]
    passage_grad = by_tensor(homes, yh, core).reshape(24, tokens, dim)
    return query_grad, passage_grad, loss


def solution(mesh):
    fine = Mesh(mesh.devices.reshape(4, 2, 4, 2, 2), ("x", "yl", "z", "yh", "c"))
    dp = ("x", "yl", "z")
    tensor = ("yh", "c")
    return jax.shard_map(
        body,
        mesh=fine,
        in_specs=(P(dp, None, None), P(dp, tensor, None), P(dp)),
        out_specs=(P(dp, None, None), P(dp, tensor, None), P()),
        check_vma=False,
    )
```

```python
import jax
import jax.numpy as jnp
import numpy as np
from jax import lax
from jax.experimental import pallas as pl
from jax.experimental.pallas import tpu as pltpu
from jax.sharding import Mesh
from jax.sharding import PartitionSpec as P

sharpness = 4.0
to_base2 = sharpness * float(np.log2(np.e))
f32 = jnp.float32
bf16 = jnp.bfloat16

chunks = (8, 4)
peers = 8
span = 24
tokens = 32
ptok = 128
dim = 128
extra = 16
lane_tile = 256
block = 1024

nt = (((1,), (1,)), ((), ()))
params = pltpu.CompilerParams(vmem_limit_bytes=36 * 2**20)
cost = pl.CostEstimate(flops=3 * 10**10, bytes_accessed=8 * 10**6, transcendentals=10**7)
smem = pl.BlockSpec(memory_space=pltpu.SMEM)
vmem = pl.BlockSpec(memory_space=pltpu.VMEM)


def absolute(place, peer):
    back, side = peer // 2, peer % 2
    return lax.rem(place[0] + side, 2) * 4 + lax.rem(place[1] + 4 - back, 4)


def chunk_rows(number):
    start = sum(c * tokens + extra for c in chunks[:number])
    lane = sum(c * tokens * peers for c in chunks[:number])
    return start, chunks[number] * tokens, lane


def load_queries(numbers, qins, qs, pos):
    first = chunk_rows(numbers[0])[2]
    for number in numbers:
        start, rows, lane = chunk_rows(number)
        for peer in range(peers):
            source = qins[peer % 2].at[peer // 2]
            here = lane - first + peer * rows
            qs[here : here + rows, :] = source[start : start + rows, :]
            tail = source[start + rows : start + rows + extra, :].astype(f32)
            for piece in range(rows // dim):
                pos[0:1, here + piece * dim : here + (piece + 1) * dim] = (
                    tail[piece : piece + 1] * 32.0 + tail[8 + piece : 9 + piece]
                )


def load_passages(pins, ps):
    for slot, pin in enumerate(pins):
        for x in range(4):
            for k in range(6):
                for part in range(4):
                    row = (slot * span + x * 6 + k) * ptok + part * tokens
                    ps[row : row + tokens, :] = pin[x * 4 + part, k * tokens : (k + 1) * tokens, :]


def group_sum(values, ones):
    high = values.astype(bf16)
    rest = values - high.astype(f32)
    middle = rest.astype(bf16)
    low = (rest - middle.astype(f32)).astype(bf16)
    dot = lambda part: jnp.dot(part, ones, preferred_element_type=f32)
    return dot(high) + (dot(middle) + dot(low))


def forward_kernel(slots, first, copies, *refs):
    refs = list(refs)
    place = refs.pop(0)
    qins = [refs.pop(0) for _ in range(2)]
    pins = [refs.pop(0) for _ in range(slots)]
    ids = [refs.pop(0) for _ in range(slots)]
    before = None if first else refs.pop(0)
    lses = [refs.pop(0) for _ in range(slots)]
    tables = [refs.pop(0) for _ in range(slots)]
    part, qs, ps, pos, ones, local = refs
    load_queries((0, 1), qins, qs, pos)
    load_passages(pins, ps)
    groups = [
        lax.shift_right_logical(lax.broadcasted_iota(jnp.int32, ones.shape, axis), 5)
        for axis in (0, 1)
    ]
    ones[...] = (groups[0] == groups[1]).astype(f32).astype(bf16)

    @pl.loop(0, qs.shape[0] // (4 * lane_tile))
    def _(step):
        for side in range(4):
            start = pl.multiple_of(step * (4 * lane_tile) + side * lane_tile, lane_tile)
            here = pl.ds(start, lane_tile)
            tile = qs[here, :]
            for i in range(slots * span):
                sims = lax.dot_general(
                    ps[i * ptok : (i + 1) * ptok, :], tile, nt, preferred_element_type=f32
                )
                top = jnp.max(sims, axis=0, keepdims=True)
                total = jnp.sum(jnp.exp2((sims - top) * to_base2), axis=0, keepdims=True)
                lses[i // span][i % span : i % span + 1, here] = top + jnp.log(total) * (
                    1.0 / sharpness
                )

    for tile in range(qs.shape[0] // lane_tile):
        here = slice(tile * lane_tile, (tile + 1) * lane_tile)
        positive = top = None
        for slot in range(slots):
            summed = group_sum(lses[slot][:, here], ones[...])
            tables[slot][:, here] = summed
            hit = pos[0:1, here] == ids[slot][...]
            found = jnp.sum(jnp.where(hit, summed, 0.0), axis=0, keepdims=True)
            most = jnp.max(summed, axis=0, keepdims=True)
            positive = found if slot == 0 else positive + found
            top = most if slot == 0 else jnp.maximum(top, most)
        if not first:
            top = jnp.maximum(top, before[0:1, here])
            positive = positive + before[1:2, here]
        total = jnp.exp(before[0:1, here] - top) if not first else 0.0
        for slot in range(slots):
            total = total + jnp.sum(jnp.exp(tables[slot][:, here] - top), axis=0, keepdims=True)
        local[0:1, here] = top + jnp.log(total)
        local[1:2, here] = positive

    if copies == 1:
        part[...] = local[...]
    else:
        for number in range(len(chunks)):
            _, rows, lane = chunk_rows(number)
            for peer in range(peers):
                start = lane + absolute(place, peer) * rows
                there = pl.ds(pl.multiple_of(start, rows), rows)
                for copy in range(copies):
                    part[copy, :, there] = local[:, lane + peer * rows : lane + (peer + 1) * rows]


def forward(place, qins, pins, ids, before, copies):
    lanes = peers * sum(chunks) * tokens
    slots = len(pins)
    first = before is None
    shapes = [(span, lanes)] * (2 * slots)
    shapes.append((2, lanes) if copies == 1 else (copies, 2, lanes))
    ops = [place, *qins, *pins, *ids] + ([] if first else [before])
    outs = pl.pallas_call(
        lambda *refs: forward_kernel(slots, first, copies, *refs),
        out_shape=[jax.ShapeDtypeStruct(s, f32) for s in shapes],
        out_specs=[vmem] * len(shapes),
        in_specs=[smem] + [vmem] * (len(ops) - 1),
        scratch_shapes=[
            pltpu.VMEM((lanes, dim), bf16),
            pltpu.VMEM((slots * span * ptok, dim), bf16),
            pltpu.VMEM((1, lanes), f32),
            pltpu.VMEM((lane_tile, lane_tile), bf16),
            pltpu.VMEM((2, lanes), f32),
        ],
        compiler_params=params,
        cost_estimate=cost,
    )(*ops)
    return outs[:slots], outs[slots : 2 * slots], outs[-1]


def aligned(value, size):
    return value if isinstance(value, int) else pl.multiple_of(value, size)


def write_payload(own, other, loss_own, loss_other, outs):
    for x in range(4):
        out = outs[x]
        for k in range(6):
            for part in range(4):
                row = (x * 6 + k) * ptok + part * tokens
                there = part * 6 * tokens + k * tokens
                out[there : there + tokens, :] = (
                    own[row : row + tokens, :] + other[row : row + tokens, :]
                ).astype(out.dtype)
    value = loss_own[...] + loss_other[...]
    high = value.astype(bf16).astype(f32)
    middle = (value - high).astype(bf16).astype(f32)
    low = value - high - middle
    which = lax.broadcasted_iota(jnp.int32, (extra, dim), 0)
    rows = jnp.where(which == 0, high[0:1], jnp.where(which == 1, middle[0:1], low[0:1]))
    for out in outs:
        out[4 * 6 * tokens :, :] = rows.astype(out.dtype)


def backward_kernel(stage, numbers, *refs):
    refs = list(refs)
    place, qa, qb, pin, ids, lse, table, gathered = refs[:8]
    del refs[:8]
    qg_in = refs.pop(0) if stage > 0 else None
    if stage == 2:
        pg_in, other, loss_own, loss_other, *outs = refs[:8]
        del refs[:8]
        qg, qs, ps, pt, pos, grad, mixed, pg = refs
    elif stage == 1:
        pg, *parts_out, qs, ps, pt, pos, grad, mixed = refs
    else:
        pg, qg, loss, qs, ps, pt, pos, grad, mixed, gap = refs
    load_queries(numbers, (qa, qb), qs, pos)
    load_passages([pin], ps)
    pt[...] = ps[...].T
    first = chunk_rows(numbers[0])[2]
    for number in numbers:
        _, rows, lane = chunk_rows(number)
        for peer in range(peers):
            there = pl.ds(pl.multiple_of(lane + absolute(place, peer) * rows, rows), rows)
            here = slice(lane - first + peer * rows, lane - first + (peer + 1) * rows)
            parts = gathered[:, 0, there]
            top = jnp.max(parts, axis=0, keepdims=True)
            row_lse = top + jnp.log(jnp.sum(jnp.exp(parts - top), axis=0, keepdims=True))
            if stage == 0:
                gap[0:1, there] = row_lse - jnp.sum(gathered[:, 1, there], axis=0, keepdims=True)
            hit = (pos[0:1, here] == ids[...]).astype(f32)
            score = table[:, lane + peer * rows : lane + (peer + 1) * rows]
            grad[:, here] = jnp.exp(score - row_lse) - hit
    if stage == 0:
        value = jnp.sum(gap[...], axis=1, keepdims=True)
        loss[...] = jnp.broadcast_to(value, loss.shape)
    pg[...] = pg_in[...] if stage == 2 else jnp.zeros_like(pg)

    def work(step):
        for piece in range(block // lane_tile):
            start = aligned(step * block + piece * lane_tile, lane_tile)
            here = pl.ds(start, lane_tile)
            there = pl.ds(aligned(first + start, lane_tile), lane_tile)
            tile = qs[here, :]
            for i in range(span):
                sims = lax.dot_general(
                    ps[i * ptok : (i + 1) * ptok, :], tile, nt, preferred_element_type=f32
                )
                weights = jnp.exp2((sims - lse[i : i + 1, there]) * to_base2)
                mixed[i * ptok : (i + 1) * ptok, piece * lane_tile : (piece + 1) * lane_tile] = (
                    weights * grad[i : i + 1, here]
                ).astype(bf16)
        whole = pl.ds(aligned(step * block, block), block)
        pg[...] += jnp.dot(mixed[...], qs[whole, :], preferred_element_type=f32)
        terms = jnp.dot(pt[...], mixed[...], preferred_element_type=f32).T
        if stage > 0:
            terms = terms + qg_in[pl.ds(aligned(first + step * block, block), block), :]
        if stage == 0:
            qg[whole, :] = terms
        elif stage == 1:
            size = parts_out[0].shape[0]
            for part in range(block // size):
                parts_out[step * (block // size) + part][...] = terms[
                    part * size : (part + 1) * size
                ].astype(bf16)
        else:
            rows = chunk_rows(numbers[0])[1]
            for part in range(block // rows):
                start = absolute(place, step * (block // rows) + part) * (2 * rows)
                piece = terms[part * rows : (part + 1) * rows].astype(qg.dtype)
                for copy in range(2):
                    qg[pl.ds(pl.multiple_of(start + copy * rows, rows), rows), :] = piece

    if stage == 0:
        pl.loop(0, qs.shape[0] // block)(work)
    else:
        for step in range(qs.shape[0] // block):
            work(step)
    if stage == 2:
        write_payload(pg, other, loss_own, loss_other, outs)


def backward(stage, *ops):
    numbers = ((0, 1), (0,), (1,))[stage]
    lanes = peers * sum(chunks[n] for n in numbers) * tokens
    shape = jax.ShapeDtypeStruct
    gradient = shape((span * ptok, dim), f32)
    payload = 4 * 6 * tokens + extra
    outs = [
        [gradient, shape((lanes, dim), f32), shape((8, dim), f32)],
        [gradient] + [shape((lanes // 4, dim), bf16)] * 4,
        [shape((payload, dim), f32 if x == 0 else bf16) for x in range(4)]
        + [shape((2 * lanes, dim), bf16)],
    ][stage]
    scratch = [
        pltpu.VMEM((lanes, dim), bf16),
        pltpu.VMEM((span * ptok, dim), bf16),
        pltpu.VMEM((dim, span * ptok), bf16),
        pltpu.VMEM((1, lanes), f32),
        pltpu.VMEM((span, lanes), f32),
        pltpu.VMEM((span * ptok, block), bf16),
    ]
    if stage == 0:
        scratch.append(pltpu.VMEM((1, lanes), f32))
    if stage == 2:
        scratch.append(pltpu.VMEM((span * ptok, dim), f32))
    return pl.pallas_call(
        lambda *refs: backward_kernel(stage, numbers, *refs),
        out_shape=outs,
        out_specs=[vmem] * len(outs),
        in_specs=[smem] + [vmem] * (len(ops) - 1),
        scratch_shapes=scratch,
        compiler_params=params,
        cost_estimate=cost,
    )(*ops)


def exchange(value, axes, step):
    size = 4 if isinstance(axes, tuple) else 2
    return lax.ppermute(value, axes, [(i, i ^ step) for i in range(size)])


def rotate(value, step):
    return lax.ppermute(value, "x", [(i, (i + step) % 4) for i in range(4)])


def by_tensor(blocks, yh, core):
    a, b, c, d = blocks
    a, b = jnp.where(core == 0, a, b), jnp.where(core == 0, b, a)
    c, d = jnp.where(core == 0, c, d), jnp.where(core == 0, d, c)
    low = [jnp.where(yh == 0, u, v) for u, v in ((a, c), (b, d), (c, a), (d, b))]
    return jnp.concatenate(low)


def body(queries, passages, positives):
    core, yh, yl, z, x = (lax.axis_index(a) for a in ("c", "yh", "yl", "z", "x"))
    spot = yh * 2 + core
    both = ("yh", "c")
    group = ("yl", "z", "yh")

    half = lax.dynamic_slice_in_dim(queries, core * 12, 12, 0)
    half_positives = lax.dynamic_slice_in_dim(positives, core * 12, 12, 0)
    pieces = []
    start = 0
    for count in chunks:
        rows = half[start : start + count].reshape(count * tokens, dim)
        spread = jnp.repeat(half_positives[start : start + count], tokens).reshape(-1, dim)
        pad = ((0, 8 - spread.shape[0]), (0, 0))
        tail = jnp.concatenate([jnp.pad(spread // 32, pad), jnp.pad(spread % 32, pad)])
        pieces += [rows, tail.astype(bf16)]
        start += count
    piece = jnp.concatenate(pieces)
    blocks = passages.reshape(4, 6 * tokens, dim)
    part_of = lambda s: lax.dynamic_slice_in_dim(blocks, spot ^ s, 1, 0)
    quarters = [part_of(0)] + [exchange(part_of(s), both, s) for s in (1, 2, 3)]
    around = [piece] + [
        lax.ppermute(piece, "z", [(i, (i + s) % 4) for i in range(4)]) for s in (1, 2, 3)
    ]
    quarters, around = lax.optimization_barrier((quarters, around))
    quarters = jnp.concatenate(quarters)
    around = jnp.stack(around)
    own = [quarters] + [rotate(quarters, s) for s in (1, 2, 3)]
    qins = [around, exchange(around, "yl", 1)]
    own, qins = lax.optimization_barrier((own, qins))
    own = jnp.concatenate(own)
    pins = [own, exchange(own, "c", 1)]
    place = jnp.stack([yl, z]).astype(jnp.int32)

    numbers = jnp.arange(span, dtype=jnp.int32)
    local = ((x + 4 - numbers // 6) % 4) * 192 + numbers % 6 + (yl * 4 + z) * 24
    ids = [(local + (spot ^ side) * 6).astype(f32)[:, None] for side in (0, 1)]

    lse0, table0, part = forward(place, qins, pins[:1], ids[:1], None, 1)
    lse1, table1, part = forward(place, qins, pins[1:], ids[1:], part, 16)
    gathered = lax.all_to_all(part, group, 0, 0, tiled=True)

    common = (place, *qins)
    own_side = (pins[0], ids[0], *lse0, *table0, gathered)
    pg1, qg1, loss = backward(0, *common, pins[1], ids[1], *lse1, *table1, gathered)
    other = exchange(pg1, "c", 1)
    loss_other = exchange(loss, "c", 1)
    pg0, *terms = backward(1, *common, *own_side, qg1)
    terms = [terms[0]] + [
        lax.ppermute(terms[s], "z", [(i, (i + 4 - s) % 4) for i in range(4)]) for s in (1, 2, 3)
    ]
    *sent, qg = backward(2, *common, *own_side, qg1, pg0, other, loss, loss_other)

    sent, terms = lax.optimization_barrier((sent, terms))
    landed = [sent[0]] + [rotate(sent[s], 4 - s) for s in (1, 2, 3)]
    terms = [t.astype(f32).reshape(2, -1, dim) for t in terms]
    early = (terms[0] + terms[1]) + (terms[2] + terms[3])
    early = early[0] + exchange(early[1], "yl", 1)
    qg, early = lax.optimization_barrier((qg, early))
    arrived = lax.all_to_all(qg.reshape(16, -1, dim), group, 0, 0, tiled=True)
    early = early + exchange(early, "yh", 1)
    landed = [part.astype(f32) for part in landed]
    summed = (landed[0] + landed[2]) + (landed[1] + landed[3])
    loss = jnp.sum(summed[4 * 6 * tokens : 4 * 6 * tokens + 3, 0]) / (768 * tokens)

    rows = 6 * tokens
    done = jnp.concatenate([early, jnp.sum(arrived.astype(f32), axis=0)])
    sibling = exchange(done, "c", 1)
    query_grad = jnp.concatenate(
        [jnp.where(core == 0, done, sibling), jnp.where(core == 0, sibling, done)]
    ).reshape(24, tokens, dim)

    homes = [summed[:rows]] + [
        exchange(summed[s * rows : (s + 1) * rows], both, s) for s in (1, 2, 3)
    ]
    passage_grad = by_tensor(homes, yh, core).reshape(24, tokens, dim)
    return query_grad, passage_grad, loss


def solution(mesh):
    fine = Mesh(mesh.devices.reshape(4, 2, 4, 2, 2), ("x", "yl", "z", "yh", "c"))
    dp = ("x", "yl", "z")
    tensor = ("yh", "c")
    return jax.shard_map(
        body,
        mesh=fine,
        in_specs=(P(dp, None, None), P(dp, tensor, None), P(dp)),
        out_specs=(P(dp, None, None), P(dp, tensor, None), P()),
        check_vma=False,
    )
```

```python
import jax
import jax.numpy as jnp
import numpy as np
from jax import lax
from jax.experimental import pallas as pl
from jax.experimental.pallas import tpu as pltpu
from jax.sharding import Mesh
from jax.sharding import PartitionSpec as P

sharpness = 4.0
to_base2 = sharpness * float(np.log2(np.e))
f32 = jnp.float32
bf16 = jnp.bfloat16

chunks = (8, 4)
peers = 8
span = 24
tokens = 32
ptok = 128
dim = 128
extra = 16
lane_tile = 256
block = 1024

nt = (((1,), (1,)), ((), ()))
params = pltpu.CompilerParams(vmem_limit_bytes=36 * 2**20)
cost = pl.CostEstimate(flops=3 * 10**10, bytes_accessed=8 * 10**6, transcendentals=10**7)
smem = pl.BlockSpec(memory_space=pltpu.SMEM)
vmem = pl.BlockSpec(memory_space=pltpu.VMEM)


def absolute(place, peer):
    back, side = peer // 2, peer % 2
    return lax.rem(place[0] + side, 2) * 4 + lax.rem(place[1] + 4 - back, 4)


def chunk_rows(number):
    start = sum(c * tokens + extra for c in chunks[:number])
    lane = sum(c * tokens * peers for c in chunks[:number])
    return start, chunks[number] * tokens, lane


def load_queries(numbers, qins, qs, pos):
    first = chunk_rows(numbers[0])[2]
    for number in numbers:
        start, rows, lane = chunk_rows(number)
        for peer in range(peers):
            source = qins[peer % 2].at[peer // 2]
            here = lane - first + peer * rows
            qs[here : here + rows, :] = source[start : start + rows, :]
            tail = source[start + rows : start + rows + extra, :].astype(f32)
            for piece in range(rows // dim):
                pos[0:1, here + piece * dim : here + (piece + 1) * dim] = (
                    tail[piece : piece + 1] * 32.0 + tail[8 + piece : 9 + piece]
                )


def load_passages(pins, ps):
    for slot, pin in enumerate(pins):
        for x in range(4):
            for k in range(6):
                for part in range(4):
                    row = (slot * span + x * 6 + k) * ptok + part * tokens
                    ps[row : row + tokens, :] = pin[x * 4 + part, k * tokens : (k + 1) * tokens, :]


def group_sum(values, ones):
    high = values.astype(bf16)
    rest = values - high.astype(f32)
    middle = rest.astype(bf16)
    low = (rest - middle.astype(f32)).astype(bf16)
    dot = lambda part: jnp.dot(part, ones, preferred_element_type=f32)
    return dot(high) + (dot(middle) + dot(low))


def forward_kernel(slots, first, copies, *refs):
    refs = list(refs)
    place = refs.pop(0)
    qins = [refs.pop(0) for _ in range(2)]
    pins = [refs.pop(0) for _ in range(slots)]
    ids = [refs.pop(0) for _ in range(slots)]
    before = None if first else refs.pop(0)
    lses = [refs.pop(0) for _ in range(slots)]
    tables = [refs.pop(0) for _ in range(slots)]
    part, qs, ps, pos, ones, local = refs
    load_queries((0, 1), qins, qs, pos)
    load_passages(pins, ps)
    groups = [
        lax.shift_right_logical(lax.broadcasted_iota(jnp.int32, ones.shape, axis), 5)
        for axis in (0, 1)
    ]
    ones[...] = (groups[0] == groups[1]).astype(f32).astype(bf16)

    @pl.loop(0, qs.shape[0] // (4 * lane_tile))
    def _(step):
        for side in range(4):
            start = pl.multiple_of(step * (4 * lane_tile) + side * lane_tile, lane_tile)
            here = pl.ds(start, lane_tile)
            tile = qs[here, :]
            for i in range(slots * span):
                sims = lax.dot_general(
                    ps[i * ptok : (i + 1) * ptok, :], tile, nt, preferred_element_type=f32
                )
                top = jnp.max(sims, axis=0, keepdims=True)
                total = jnp.sum(jnp.exp2((sims - top) * to_base2), axis=0, keepdims=True)
                lses[i // span][i % span : i % span + 1, here] = top + jnp.log(total) * (
                    1.0 / sharpness
                )

    for tile in range(qs.shape[0] // lane_tile):
        here = slice(tile * lane_tile, (tile + 1) * lane_tile)
        positive = top = None
        for slot in range(slots):
            summed = group_sum(lses[slot][:, here], ones[...])
            tables[slot][:, here] = summed
            hit = pos[0:1, here] == ids[slot][...]
            found = jnp.sum(jnp.where(hit, summed, 0.0), axis=0, keepdims=True)
            most = jnp.max(summed, axis=0, keepdims=True)
            positive = found if slot == 0 else positive + found
            top = most if slot == 0 else jnp.maximum(top, most)
        if not first:
            top = jnp.maximum(top, before[0:1, here])
            positive = positive + before[1:2, here]
        total = jnp.exp(before[0:1, here] - top) if not first else 0.0
        for slot in range(slots):
            total = total + jnp.sum(jnp.exp(tables[slot][:, here] - top), axis=0, keepdims=True)
        local[0:1, here] = top + jnp.log(total)
        local[1:2, here] = positive

    if copies == 1:
        part[...] = local[...]
    else:
        for number in range(len(chunks)):
            _, rows, lane = chunk_rows(number)
            for peer in range(peers):
                start = lane + absolute(place, peer) * rows
                there = pl.ds(pl.multiple_of(start, rows), rows)
                for copy in range(copies):
                    part[copy, :, there] = local[:, lane + peer * rows : lane + (peer + 1) * rows]


def forward(place, qins, pins, ids, before, copies):
    lanes = peers * sum(chunks) * tokens
    slots = len(pins)
    first = before is None
    shapes = [(span, lanes)] * (2 * slots)
    shapes.append((2, lanes) if copies == 1 else (copies, 2, lanes))
    ops = [place, *qins, *pins, *ids] + ([] if first else [before])
    outs = pl.pallas_call(
        lambda *refs: forward_kernel(slots, first, copies, *refs),
        out_shape=[jax.ShapeDtypeStruct(s, f32) for s in shapes],
        out_specs=[vmem] * len(shapes),
        in_specs=[smem] + [vmem] * (len(ops) - 1),
        scratch_shapes=[
            pltpu.VMEM((lanes, dim), bf16),
            pltpu.VMEM((slots * span * ptok, dim), bf16),
            pltpu.VMEM((1, lanes), f32),
            pltpu.VMEM((lane_tile, lane_tile), bf16),
            pltpu.VMEM((2, lanes), f32),
        ],
        compiler_params=params,
        cost_estimate=cost,
    )(*ops)
    return outs[:slots], outs[slots : 2 * slots], outs[-1]


def aligned(value, size):
    return value if isinstance(value, int) else pl.multiple_of(value, size)


def write_payload(own, other, loss_own, loss_other, outs):
    for x in range(4):
        out = outs[x]
        for k in range(6):
            for part in range(4):
                row = (x * 6 + k) * ptok + part * tokens
                there = part * 6 * tokens + k * tokens
                out[there : there + tokens, :] = (
                    own[row : row + tokens, :] + other[row : row + tokens, :]
                ).astype(out.dtype)
    value = loss_own[...] + loss_other[...]
    high = value.astype(bf16).astype(f32)
    middle = (value - high).astype(bf16).astype(f32)
    low = value - high - middle
    which = lax.broadcasted_iota(jnp.int32, (extra, dim), 0)
    rows = jnp.where(which == 0, high[0:1], jnp.where(which == 1, middle[0:1], low[0:1]))
    for out in outs:
        out[4 * 6 * tokens :, :] = rows.astype(out.dtype)


def backward_kernel(stage, numbers, *refs):
    refs = list(refs)
    place, qa, qb, pin, ids, lse, table, gathered = refs[:8]
    del refs[:8]
    qg_in = refs.pop(0) if stage > 0 else None
    if stage == 2:
        pg_in, other, loss_own, loss_other, *outs = refs[:8]
        del refs[:8]
        qg, qs, ps, pt, pos, grad, mixed, pg = refs
    elif stage == 1:
        pg, *parts_out, qs, ps, pt, pos, grad, mixed = refs
    else:
        pg, qg, loss, qs, ps, pt, pos, grad, mixed, gap = refs
    load_queries(numbers, (qa, qb), qs, pos)
    load_passages([pin], ps)
    pt[...] = ps[...].T
    first = chunk_rows(numbers[0])[2]
    for number in numbers:
        _, rows, lane = chunk_rows(number)
        for peer in range(peers):
            there = pl.ds(pl.multiple_of(lane + absolute(place, peer) * rows, rows), rows)
            here = slice(lane - first + peer * rows, lane - first + (peer + 1) * rows)
            parts = gathered[:, 0, there]
            top = jnp.max(parts, axis=0, keepdims=True)
            row_lse = top + jnp.log(jnp.sum(jnp.exp(parts - top), axis=0, keepdims=True))
            if stage == 0:
                gap[0:1, there] = row_lse - jnp.sum(gathered[:, 1, there], axis=0, keepdims=True)
            hit = (pos[0:1, here] == ids[...]).astype(f32)
            score = table[:, lane + peer * rows : lane + (peer + 1) * rows]
            grad[:, here] = jnp.exp(score - row_lse) - hit
    if stage == 0:
        value = jnp.sum(gap[...], axis=1, keepdims=True)
        loss[...] = jnp.broadcast_to(value, loss.shape)
    pg[...] = pg_in[...] if stage == 2 else jnp.zeros_like(pg)

    def work(step):
        for piece in range(block // lane_tile):
            start = aligned(step * block + piece * lane_tile, lane_tile)
            here = pl.ds(start, lane_tile)
            there = pl.ds(aligned(first + start, lane_tile), lane_tile)
            tile = qs[here, :]
            for i in range(span):
                sims = lax.dot_general(
                    ps[i * ptok : (i + 1) * ptok, :], tile, nt, preferred_element_type=f32
                )
                weights = jnp.exp2((sims - lse[i : i + 1, there]) * to_base2)
                mixed[i * ptok : (i + 1) * ptok, piece * lane_tile : (piece + 1) * lane_tile] = (
                    weights * grad[i : i + 1, here]
                ).astype(bf16)
        whole = pl.ds(aligned(step * block, block), block)
        pg[...] += jnp.dot(mixed[...], qs[whole, :], preferred_element_type=f32)
        terms = jnp.dot(pt[...], mixed[...], preferred_element_type=f32).T
        if stage > 0:
            terms = terms + qg_in[pl.ds(aligned(first + step * block, block), block), :]
        if stage == 0:
            qg[whole, :] = terms
        elif stage == 1:
            size = parts_out[0].shape[0]
            for part in range(block // size):
                parts_out[step * (block // size) + part][...] = terms[
                    part * size : (part + 1) * size
                ].astype(bf16)
        else:
            rows = chunk_rows(numbers[0])[1]
            for part in range(block // rows):
                start = absolute(place, step * (block // rows) + part) * (2 * rows)
                piece = terms[part * rows : (part + 1) * rows].astype(qg.dtype)
                for copy in range(2):
                    qg[pl.ds(pl.multiple_of(start + copy * rows, rows), rows), :] = piece

    if stage == 0:
        pl.loop(0, qs.shape[0] // block)(work)
    else:
        for step in range(qs.shape[0] // block):
            work(step)
    if stage == 2:
        write_payload(pg, other, loss_own, loss_other, outs)


def backward(stage, *ops):
    numbers = ((0, 1), (0,), (1,))[stage]
    lanes = peers * sum(chunks[n] for n in numbers) * tokens
    shape = jax.ShapeDtypeStruct
    gradient = shape((span * ptok, dim), f32)
    payload = 4 * 6 * tokens + extra
    outs = [
        [gradient, shape((lanes, dim), f32), shape((8, dim), f32)],
        [gradient] + [shape((lanes // 4, dim), bf16)] * 4,
        [shape((payload, dim), f32 if x == 0 else bf16) for x in range(4)]
        + [shape((2 * lanes, dim), bf16)],
    ][stage]
    scratch = [
        pltpu.VMEM((lanes, dim), bf16),
        pltpu.VMEM((span * ptok, dim), bf16),
        pltpu.VMEM((dim, span * ptok), bf16),
        pltpu.VMEM((1, lanes), f32),
        pltpu.VMEM((span, lanes), f32),
        pltpu.VMEM((span * ptok, block), bf16),
    ]
    if stage == 0:
        scratch.append(pltpu.VMEM((1, lanes), f32))
    if stage == 2:
        scratch.append(pltpu.VMEM((span * ptok, dim), f32))
    return pl.pallas_call(
        lambda *refs: backward_kernel(stage, numbers, *refs),
        out_shape=outs,
        out_specs=[vmem] * len(outs),
        in_specs=[smem] + [vmem] * (len(ops) - 1),
        scratch_shapes=scratch,
        compiler_params=params,
        cost_estimate=cost,
    )(*ops)


def exchange(value, axes, step):
    size = 4 if isinstance(axes, tuple) else 2
    return lax.ppermute(value, axes, [(i, i ^ step) for i in range(size)])


def rotate(value, step):
    return lax.ppermute(value, "x", [(i, (i + step) % 4) for i in range(4)])


def by_tensor(blocks, yh, core):
    a, b, c, d = blocks
    a, b = jnp.where(core == 0, a, b), jnp.where(core == 0, b, a)
    c, d = jnp.where(core == 0, c, d), jnp.where(core == 0, d, c)
    low = [jnp.where(yh == 0, u, v) for u, v in ((a, c), (b, d), (c, a), (d, b))]
    return jnp.concatenate(low)


def body(queries, passages, positives):
    core, yh, yl, z, x = (lax.axis_index(a) for a in ("c", "yh", "yl", "z", "x"))
    spot = yh * 2 + core
    both = ("yh", "c")
    group = ("yl", "z", "yh")

    half = lax.dynamic_slice_in_dim(queries, core * 12, 12, 0)
    half_positives = lax.dynamic_slice_in_dim(positives, core * 12, 12, 0)
    pieces = []
    start = 0
    for count in chunks:
        rows = half[start : start + count].reshape(count * tokens, dim)
        spread = jnp.repeat(half_positives[start : start + count], tokens).reshape(-1, dim)
        pad = ((0, 8 - spread.shape[0]), (0, 0))
        tail = jnp.concatenate([jnp.pad(spread // 32, pad), jnp.pad(spread % 32, pad)])
        pieces += [rows, tail.astype(bf16)]
        start += count
    piece = jnp.concatenate(pieces)
    blocks = passages.reshape(4, 6 * tokens, dim)
    part_of = lambda s: lax.dynamic_slice_in_dim(blocks, spot ^ s, 1, 0)
    quarters = [part_of(0)] + [exchange(part_of(s), both, s) for s in (1, 2, 3)]
    around = [piece] + [
        lax.ppermute(piece, "z", [(i, (i + s) % 4) for i in range(4)]) for s in (1, 2, 3)
    ]
    quarters, around = lax.optimization_barrier((quarters, around))
    quarters = jnp.concatenate(quarters)
    around = jnp.stack(around)
    own = [quarters] + [rotate(quarters, s) for s in (1, 2, 3)]
    qins = [around, exchange(around, "yl", 1)]
    own, qins = lax.optimization_barrier((own, qins))
    own = jnp.concatenate(own)
    pins = [own, exchange(own, "c", 1)]
    place = jnp.stack([yl, z]).astype(jnp.int32)

    numbers = jnp.arange(span, dtype=jnp.int32)
    local = ((x + 4 - numbers // 6) % 4) * 192 + numbers % 6 + (yl * 4 + z) * 24
    ids = [(local + (spot ^ side) * 6).astype(f32)[:, None] for side in (0, 1)]

    lse0, table0, part = forward(place, qins, pins[:1], ids[:1], None, 1)
    lse1, table1, part = forward(place, qins, pins[1:], ids[1:], part, 16)
    gathered = lax.all_to_all(part, group, 0, 0, tiled=True)

    common = (place, *qins)
    own_side = (pins[0], ids[0], *lse0, *table0, gathered)
    pg1, qg1, loss = backward(0, *common, pins[1], ids[1], *lse1, *table1, gathered)
    other = exchange(pg1, "c", 1)
    loss_other = exchange(loss, "c", 1)
    pg0, *terms = backward(1, *common, *own_side, qg1)
    terms = [terms[0]] + [
        lax.ppermute(terms[s], "z", [(i, (i + 4 - s) % 4) for i in range(4)]) for s in (1, 2, 3)
    ]
    *sent, qg = backward(2, *common, *own_side, qg1, pg0, other, loss, loss_other)

    sent, terms[1], terms[3] = lax.optimization_barrier((sent, terms[1], terms[3]))
    landed = [sent[0]] + [rotate(sent[s], 4 - s) for s in (1, 2, 3)]
    terms = [t.astype(f32).reshape(2, -1, dim) for t in terms]
    early = (terms[0] + terms[1]) + (terms[2] + terms[3])
    early = early[0] + exchange(early[1], "yl", 1)
    qg, early = lax.optimization_barrier((qg, early))
    arrived = lax.all_to_all(qg.reshape(16, -1, dim), group, 0, 0, tiled=True)
    early = early + exchange(early, "yh", 1)
    landed = [part.astype(f32) for part in landed]
    summed = (landed[0] + landed[2]) + (landed[1] + landed[3])
    loss = jnp.sum(summed[4 * 6 * tokens : 4 * 6 * tokens + 3, 0]) / (768 * tokens)

    rows = 6 * tokens
    done = jnp.concatenate([early, jnp.sum(arrived.astype(f32), axis=0)])
    sibling = exchange(done, "c", 1)
    query_grad = jnp.concatenate(
        [jnp.where(core == 0, done, sibling), jnp.where(core == 0, sibling, done)]
    ).reshape(24, tokens, dim)

    homes = [summed[:rows]] + [
        exchange(summed[s * rows : (s + 1) * rows], both, s) for s in (1, 2, 3)
    ]
    passage_grad = by_tensor(homes, yh, core).reshape(24, tokens, dim)
    return query_grad, passage_grad, loss


def solution(mesh):
    fine = Mesh(mesh.devices.reshape(4, 2, 4, 2, 2), ("x", "yl", "z", "yh", "c"))
    dp = ("x", "yl", "z")
    tensor = ("yh", "c")
    return jax.shard_map(
        body,
        mesh=fine,
        in_specs=(P(dp, None, None), P(dp, tensor, None), P(dp)),
        out_specs=(P(dp, None, None), P(dp, tensor, None), P()),
        check_vma=False,
    )
```
